32 devices in a mesh: row: 4 (over y, x), col: 8 (over z, core).
Axes of the slice: x: 2, y: 2, z: 4, core: 2. Of those that a mesh axis runs over, the one named last changes fastest.
Arguments:
- forward_state: bfloat16 [16777216], P(('row', 'col')), may hold values from -6 to 6
- adjoint_state: bfloat16 [16777216], P(('row', 'col')), may hold values from -6 to 6
- gate_matrix: bfloat16 [1024, 1024], replicated, may hold values from -1 to 1, as said below
Outputs:
- forward_final: bfloat16 [16777216], P(('row', 'col'))
- adjoint_final: bfloat16 [16777216], P(('row', 'col'))
- first_environment: float32 [1048576], P(('row', 'col'))
- second_environment: float32 [1048576], P(('row', 'col'))
The draws below stay inside these ranges and needn't reach their ends.
Inputs may be any that keep to these rules, and one draw needn't show every extreme that they name: `gate_matrix`: an orthogonal matrix rounded to bfloat16.
All inputs are finite; a program needn't handle non-finite values.
Results may differ from the reference program's by a relative error of at most 0.0057.
Values may be sent and summed in bfloat16 or wider, within the bound.
No kernel may reach another device: no remote copies, remote signals or barrier semaphores. Data moves between devices by JAX's collectives and lax.ppermute only.
A program may use at most 128 MiB of HBM per device.

```python
import math
import jax
import jax.numpy as jnp
from jax import lax

GATE = 1024
AMP_DEV = 524288
AMPS = 16777216
N_ROW = 4
N_COL = 8


def draw_gate_matrix(key, part):
    sample = jax.random.normal(jax.random.fold_in(key, 7), (GATE, GATE), jnp.float32)
    orthogonal, triangle = jnp.linalg.qr(sample)
    sign_flip = jnp.where(jnp.diagonal(triangle) < 0, -1.0, 1.0)
    return (orthogonal * sign_flip[None, :]).astype(jnp.bfloat16)


def steps_of(rng, extent, shards, least, high):
    level = 1.0
    for position, blocks in shards:
        steps = jax.random.uniform(jax.random.fold_in(jax.random.fold_in(rng, 6), position), (blocks,), jnp.float32, least / len(shards), high / len(shards))
        level = level * jnp.repeat(jnp.exp(steps), extent[position] // blocks).reshape((-1,) + (1,) * (len(extent) - 1 - position))
    return level


def centred(rng, dims, spread, bound, pieces=(), dtype=jnp.bfloat16):
    result = jax.random.normal(rng, dims, jnp.float32) * spread
    if len(pieces) > 0:
        result = steps_of(rng, dims, pieces, -0.22, 0.18) * result
    return jnp.clip(result, min=-bound, max=bound).astype(dtype)


def setup_inputs(seed: int = 0) -> dict:
    key_of = jax.random.split(jax.random.key(seed), 4)
    return {
        "forward_state": centred(key_of[0], (AMPS,), 1.0, 6.0, ((0, 32),)),
        "adjoint_state": centred(key_of[1], (AMPS,), 1.0, 6.0, ((0, 32),)),
        "gate_matrix": draw_gate_matrix(jax.random.fold_in(key_of[3], 71), 0),
    }


def gate_layer(forward, adjoint, unitary, shape, move_form, env_form, scale):
    forward_grid = forward.astype(jnp.float32).reshape(shape)
    adjoint_grid = adjoint.astype(jnp.float32).reshape(shape)
    forward_next = jnp.einsum(move_form, unitary, forward_grid, precision=lax.Precision.HIGHEST).astype(jnp.bfloat16)
    adjoint_next = jnp.einsum(move_form, unitary, adjoint_grid, precision=lax.Precision.HIGHEST).astype(jnp.bfloat16)
    environment = jnp.einsum(env_form, adjoint_next.astype(jnp.float32), forward_grid, precision=lax.Precision.HIGHEST)
    environment = (environment * scale).reshape(GATE * GATE)
    return (forward_next.reshape(-1), adjoint_next.reshape(-1), environment)

def reference(forward_state, adjoint_state, gate_matrix):
    half_row = N_ROW // 2
    half_col = N_COL // 2
    quarter = GATE // 4
    columns = AMP_DEV // GATE
    unitary = gate_matrix.astype(jnp.float32).reshape(2, 2, quarter, 2, 2, quarter)
    scale = 1.0 / math.sqrt(N_ROW * N_COL * AMP_DEV / GATE)
    first_shape = (half_row, 2, 2, half_col, 4, quarter, columns)
    forward_mid, adjoint_mid, first_environment = gate_layer(forward_state, adjoint_state, unitary, first_shape, 'ijkIJK,hIJcpKm->hijcpkm', 'hijcpkm,hIJcpKm->ijkIJK', scale)
    second_shape = (half_row, 2, half_col, 2, 4, quarter, columns)
    forward_final, adjoint_final, second_environment = gate_layer(forward_mid, adjoint_mid, unitary, second_shape, 'ijkIJK,hIcJpKm->hicjpkm', 'hicjpkm,hIcJpKm->ijkIJK', scale)
    return (forward_final, adjoint_final, first_environment, second_environment)
```

```python
import functools
import math

import jax
import jax.numpy as jnp
from jax import lax
from jax.experimental import pallas as pl
from jax.experimental.pallas import tpu as pltpu
from jax.sharding import PartitionSpec as P

AXES = ("row", "col")


def sent(value, target):
    count = lax.axis_size("row") * lax.axis_size("col")
    return lax.ppermute(value, AXES, [(i, target(i)) for i in range(count)])


def gate_kernel(block, col_ref, row_ref, gate_ref, *refs, n_in):
    state_refs, out_refs = refs[:n_in], refs[n_in:]

    def source(n):
        per = state_refs[0].shape[0] // block
        return state_refs[n // per][pl.ds(n % per * block, block), :]

    per_out = out_refs[0].shape[0] // block
    for m in range(per_out * len(out_refs)):
        rows = pl.ds(pl.multiple_of(row_ref[m] * block, block), block)
        total = None
        for n in range(4):
            cols = pl.ds(pl.multiple_of(col_ref[n] * block, block), block)
            term = jnp.dot(gate_ref[rows, cols], source(n), preferred_element_type=jnp.float32)
            total = term if total is None else total + term
        out_refs[m // per_out][pl.ds(m % per_out * block, block), :] = total.astype(jnp.bfloat16)


def apply_gate(gate_matrix, states, in_place, out_place, n_out):
    block = gate_matrix.shape[0] // 4
    width = states[0].shape[1]
    shape = jax.ShapeDtypeStruct((4 * block // n_out, width), jnp.bfloat16)
    smem = pl.BlockSpec(memory_space=pltpu.SMEM)
    vmem = pl.BlockSpec(memory_space=pltpu.VMEM)
    return pl.pallas_call(
        functools.partial(gate_kernel, block, n_in=len(states)),
        out_shape=[shape] * n_out,
        in_specs=[smem, smem] + [vmem] * (1 + len(states)),
        out_specs=[vmem] * n_out,
        compiler_params=pltpu.CompilerParams(vmem_limit_bytes=40 * 2**20),
        cost_estimate=pl.CostEstimate(
            flops=2 * 16 * block * block * width, bytes_accessed=32 * block * block + 16 * block * width, transcendentals=0
        ),
    )(in_place, out_place, gate_matrix, *states)


def env_kernel(block, part, scale, row_ref, col_ref, own_ref, *refs, n_left, n_right):
    left_refs, right_refs = refs[:n_left], refs[n_left : n_left + n_right]
    keep_ref, send_ref = refs[n_left + n_right :]
    own = own_ref[0]

    def pick(group, n):
        per = group[0].shape[0] // block
        return group[n // per][pl.ds(n % per * block, block), :]

    for m in range(4):
        rows = pl.ds(pl.multiple_of(row_ref[m] * (block // 2), block // 2), block // 2)
        for n in range(4):
            cols = pl.ds(pl.multiple_of(col_ref[n] * block, block), block)
            value = lax.dot_general(
                pick(left_refs, m), pick(right_refs, n), (((1,), (1,)), ((), ())), preferred_element_type=jnp.float32
            )
            value = (value * scale).reshape(block // (2 * part), 2, part, block)
            low, high = value[:, 0].reshape(block // 2, block), value[:, 1].reshape(block // 2, block)
            keep_ref[rows, cols] = jnp.where(own == 0, low, high)
            send_ref[rows, cols] = jnp.where(own == 0, high, low).astype(jnp.bfloat16)


def environment(left, right, left_place, right_place, own, part, scale):
    block = sum(one.shape[0] for one in left) // 4
    width = left[0].shape[1]
    smem = pl.BlockSpec(memory_space=pltpu.SMEM)
    vmem = pl.BlockSpec(memory_space=pltpu.VMEM)
    return pl.pallas_call(
        functools.partial(env_kernel, block, part, scale, n_left=len(left), n_right=len(right)),
        out_shape=[
            jax.ShapeDtypeStruct((2 * block, 4 * block), jnp.float32),
            jax.ShapeDtypeStruct((2 * block, 4 * block), jnp.bfloat16),
        ],
        in_specs=[smem] * 3 + [vmem] * (len(left) + len(right)),
        out_specs=[vmem, vmem],
        compiler_params=pltpu.CompilerParams(vmem_limit_bytes=40 * 2**20),
        cost_estimate=pl.CostEstimate(
            flops=2 * 16 * block * block * width, bytes_accessed=48 * block * block + 16 * block * width, transcendentals=0
        ),
    )(left_place, right_place, own.reshape(1), *left, *right)


def exchange_sum(value, bits, me):
    low, count = bits[0], 2 ** len(bits)
    mine = (me >> low) % count
    rows = value.shape[0] // count

    def piece(which):
        return lax.dynamic_slice_in_dim(value, which * rows, rows, 0)

    outgoing = [piece(mine ^ k).astype(jnp.bfloat16) for k in range(1, count)]
    incoming = [sent(one, lambda i, k=k: i ^ (k << low)) for k, one in enumerate(outgoing, 1)]
    total = piece(mine)
    for one in incoming:
        total = total + one.astype(jnp.float32)
    return total


def finish_environment(keep, send, me, row_bits, col_bits):
    total = keep + sent(send, lambda i: i ^ 1).astype(jnp.float32)
    total = exchange_sum(total, list(range(col_bits, col_bits + row_bits)), me)
    for bit in range(1, col_bits - 1):
        lead = 2 ** (col_bits - 1 - bit)
        rows = total.shape[0]
        grid = total.reshape(lead, 2, rows // (2 * lead), -1)
        grid = jnp.swapaxes(grid, 0, 1).reshape(rows, -1)
        total = exchange_sum(grid, [bit], me)
    if col_bits > 1:
        total = exchange_sum(total, [col_bits - 1], me)
    return total.reshape(-1)


def on_device(forward_state, adjoint_state, gate_matrix):
    row_count, col_count = lax.axis_size("row"), lax.axis_size("col")
    row_bits, col_bits = row_count.bit_length() - 1, col_count.bit_length() - 1
    me = lax.axis_index("row") * col_count + lax.axis_index("col")
    top, side = col_bits - 1, col_bits
    p, q, e = (me >> side) & 1, (me >> top) & 1, me & 1
    gate = gate_matrix.shape[0]
    block = gate // 4
    local = forward_state.shape[0]
    quarter = local // 4
    width = quarter // block
    scale = 1.0 / math.sqrt(row_count * col_count * local / gate)
    part = gate // (row_count * col_count)

    def across_x(value):
        return sent(value, lambda i: i ^ (1 << side))

    def across_z(value):
        return sent(value, lambda i: i ^ (1 << top))

    def across_core(value):
        return sent(value, lambda i: i ^ 1)

    def home(value, flip):
        return sent(value, lambda i: (i ^ ((i & 1) << top)) ^ flip)

    def arrive(state):
        def take(i, j):
            return lax.dynamic_slice_in_dim(state, ((p ^ i) * 2 + (q ^ j)) * quarter, quarter, 0)

        through = across_x(take(1, 1))
        direct = across_z(take(0, 1))
        beside = across_x(take(1, 0))
        through = across_z(through)
        return [one.reshape(block, width) for one in (take(0, 0), direct, beside, through)]

    forward_in = arrive(forward_state)
    adjoint_in = arrive(adjoint_state)
    first_in = jnp.stack([p * 2 + q, p * 2 + (1 - q), (1 - p) * 2 + q, (1 - p) * 2 + (1 - q)])
    kept = q ^ e
    first_out = jnp.stack([kept, 2 + kept, 1 - kept, 3 - kept])
    second_in = jnp.stack([e, 2 + e, 1 - e, 3 - e])
    second_out = jnp.stack([p * 2 + e, p * 2 + 1 - e, (1 - p) * 2 + e, (1 - p) * 2 + 1 - e])

    def middle(blocks):
        keep, send = apply_gate(gate_matrix, blocks, first_in, first_out, 2)
        return keep, send

    def leave(final):
        near, far = (one.reshape(-1) for one in final)
        far = across_x(far)
        result = jnp.zeros((local,), jnp.bfloat16)
        for i, one in enumerate((near, far)):
            for flip in range(2):
                got = home(one[flip * quarter : (flip + 1) * quarter], flip)
                place = (p ^ i) * 2 + (q ^ e ^ flip)
                result = lax.dynamic_update_slice_in_dim(result, got, place * quarter, 0)
        return result

    forward_keep, forward_send = middle(forward_in)
    forward_mid = [forward_keep, across_core(forward_send)]
    forward_out = apply_gate(gate_matrix, forward_mid, second_in, second_out, 2)
    forward_final = leave(forward_out)

    adjoint_keep, adjoint_send = middle(adjoint_in)
    first = environment([adjoint_keep, adjoint_send], forward_in, first_out, first_in, e, part, scale)
    adjoint_mid = [adjoint_keep, across_core(adjoint_send)]
    adjoint_out = apply_gate(gate_matrix, adjoint_mid, second_in, second_out, 2)
    second = environment(adjoint_out, forward_mid, second_out, second_in, e, part, scale)
    adjoint_final = leave(adjoint_out)

    first_environment = finish_environment(*first, me, row_bits, col_bits)
    second_environment = finish_environment(*second, me, row_bits, col_bits)
    return forward_final, adjoint_final, first_environment, second_environment


def solution(mesh):
    in_specs = (P(AXES), P(AXES), P())
    out_specs = (P(AXES),) * 4
    return jax.shard_map(on_device, mesh=mesh, in_specs=in_specs, out_specs=out_specs, check_vma=False)
```

```python
import functools
import math

import jax
import jax.numpy as jnp
from jax import lax
from jax.experimental import pallas as pl
from jax.experimental.pallas import tpu as pltpu
from jax.sharding import PartitionSpec as P

AXES = ("row", "col")
LANES = 128
KNOBS = {'waits': {'take2': ['Z1', 'Z2'], 'f_pack': ['Z3', 'f_X'], 'F2_0': ['f_near'], 'F1_1': ['a_X']}, 'lead': {'take2': 20000000000, 'F2_0': 12000000000}, 'free': ['take2'], 'out_f': 'packed', 'core_cuts': 4, 'env_cuts': 1, 'plan': '1G21212fa12', 'out_a': 'packed'}


SMEM = pl.BlockSpec(memory_space=pltpu.SMEM)
VMEM = pl.BlockSpec(memory_space=pltpu.VMEM)
HBM = pl.BlockSpec(memory_space=pltpu.HBM)
ANY = pl.BlockSpec(memory_space=pl.ANY)
VMEM_BYTES = 16 * 2**20
CORE_CUTS = KNOBS.get("core_cuts", 1)
ENV_CUTS = KNOBS.get("env_cuts", 1)


def sent(value, target):
    count = lax.axis_size("row") * lax.axis_size("col")
    return lax.ppermute(value, AXES, [(i, target(i)) for i in range(count)])

TOKEN = jax.ShapeDtypeStruct((8, LANES), jnp.float32)


def call(kernel, shapes, ids, arrays, after=(), scratch=(), raw_in=(), raw_out=(), work=0):
    n_in, n_out, n_after = len(arrays), len(shapes), len(after)

    def body(ids_ref, *refs):
        ins, refs = refs[:n_in], refs[n_in + n_after :]
        kernel([ids_ref[k] for k in range(4)], ins, refs[:n_out], *refs[n_out + 1 :])

    *results, token = pl.pallas_call(
        body,
        out_shape=[*shapes, TOKEN],
        in_specs=[SMEM] + [HBM if k in raw_in else VMEM for k in range(n_in)] + [ANY] * n_after,
        out_specs=[HBM if k in raw_out else VMEM for k in range(n_out)] + [ANY],
        scratch_shapes=list(scratch),
        compiler_params=pltpu.CompilerParams(vmem_limit_bytes=VMEM_BYTES),
        cost_estimate=pl.CostEstimate(flops=work, bytes_accessed=0, transcendentals=0),
    )(ids, *arrays, *after)
    return results, token


def arrived(ids, values, after=(), work=0):
    return call(lambda ids, ins, outs: None, [], ids, [], [*values, *after], work=work)[1]


def quarter_at(ids, i, j):
    return (ids[0] ^ i) * 2 + (ids[1] ^ j)


def take(ids, wanted, after=()):
    states = []
    for pieces in wanted:
        for one in pieces:
            if isinstance(one, tuple) and not any(one[0] is state for state in states):
                states.append(one[0])
    rows = states[0].shape[0] // 4
    arrays = [one for pieces in wanted for one in pieces if not isinstance(one, tuple)]
    plan = []
    for k, pieces in enumerate(wanted):
        for n, one in enumerate(pieces):
            if isinstance(one, tuple):
                plan.append((k, n, next(i for i, state in enumerate(states) if state is one[0]), one[1:]))
            else:
                plan.append((k, n, next(i for i, other in enumerate(arrays) if other is one), None))
    count = sum(at is not None for *_, at in plan)

    def kernel(ids, ins, outs, sems):
        copies = []
        for k, n, i, at in plan:
            if at is not None:
                start = pl.multiple_of(quarter_at(ids, *at) * rows, rows)
                target = outs[k].at[pl.ds(n * rows, rows)]
                copies.append(pltpu.make_async_copy(ins[i].at[pl.ds(start, rows)], target, sems.at[len(copies)]))
                copies[-1].start()
        for k, n, i, at in plan:
            if at is None:
                outs[k][n * rows : (n + 1) * rows, :] = ins[len(states) + i][...]
        for copy in copies:
            copy.wait()

    shapes = [jax.ShapeDtypeStruct((rows * len(pieces), LANES), states[0].dtype) for pieces in wanted]
    scratch = [pltpu.SemaphoreType.DMA((count,))]
    return call(kernel, shapes, ids, states + arrays, after, scratch, raw_in=range(len(states)))


def put(ids, pieces, places, after):
    count = 4
    rows = sum(piece.shape[0] for piece in pieces) // count

    def kernel(ids, ins, outs, sems):
        copies, at = [], places(ids)
        for piece in ins:
            for k in range(0, piece.shape[0], rows):
                start = pl.multiple_of(at[len(copies)] * rows, rows)
                target = outs[0].at[pl.ds(start, rows)]
                copies.append(pltpu.make_async_copy(piece.at[pl.ds(k, rows)], target, sems.at[len(copies)]))
                copies[-1].start()
        for copy in copies:
            copy.wait()

    shapes = [jax.ShapeDtypeStruct((rows * count, LANES), pieces[0].dtype)]
    scratch = [pltpu.SemaphoreType.DMA((count,))]
    return call(kernel, shapes, ids, pieces, after, scratch, raw_out=[0])


def pack(ids, groups, after):
    arrays = [one for group in groups for one in group]

    def kernel(ids, ins, outs):
        count = 0
        for group, out in zip(groups, outs, strict=True):
            row = 0
            for one in group:
                out[row : row + one.shape[0], :] = ins[count][...]
                row += one.shape[0]
                count += 1

    shapes = [jax.ShapeDtypeStruct((sum(one.shape[0] for one in group), LANES), group[0].dtype) for group in groups]
    return call(kernel, shapes, ids, arrays, after)


def load_state(block, linear, states, place_ref, moved_ref, spread):
    ratio = moved_ref.shape[1] // LANES
    if linear:
        lines, n = block * ratio, 0
        for state in states:
            for k in range(0, state.shape[0], lines):
                rows = pl.ds(pl.multiple_of(place_ref[n] * block, block), block)
                spread[...] = state[k : k + lines, :].astype(jnp.float32)
                for c in range(ratio):
                    part = spread[pl.ds(c, block, stride=ratio), :]
                    moved_ref[rows, c * LANES : (c + 1) * LANES] = part.astype(jnp.bfloat16)
                n += 1
        return
    row = 0
    for state in states:
        step = min(block, state.shape[0])
        for k in range(0, state.shape[0], step):
            start = pl.multiple_of(place_ref[row // block] * block + row % block, step)
            moved_ref[pl.ds(start, step), :] = state[k : k + step, :]
            row += step


def gate_kernel(block, linear, sizes, env, in_place, out_place, ids, ins, results, moved_ref, *refs):
    in_ref, out_ref = in_place(ids), out_place(ids)
    n_out = 4 if sizes is None else len(sizes)
    outs = results[:n_out]
    spread = refs[0]
    if env is None:
        *states, gate_ref = ins
        moved_ref = results[n_out]
    else:
        *states, other_ref, gate_ref = ins
        grid_ref, env_spread = refs[1], refs[2]
    ratio = moved_ref.shape[1] // LANES
    load_state(block, linear, states, in_ref, moved_ref, spread)
    for m in range(4):
        rows = pl.ds(pl.multiple_of(out_ref[m] * block, block), block)
        total = jnp.dot(gate_ref[rows, :], moved_ref[...], preferred_element_type=jnp.float32)
        rounded = total.astype(jnp.bfloat16)
        if env is not None:
            grid_ref[m * block : (m + 1) * block, :] = rounded
        if sizes is None:
            for c in range(ratio):
                spread[pl.ds(c, block, stride=ratio), :] = total[:, c * LANES : (c + 1) * LANES]
            outs[m][...] = spread[...].astype(jnp.bfloat16)
            continue
        row = 0
        for out in outs:
            first, last = max(row, m * block), min(row + out.shape[0], (m + 1) * block)
            if first < last:
                out[first - row : last - row, :] = rounded[first - m * block : last - m * block, :]
            row += out.shape[0]
    if env is not None:
        env_from, unit, scale = env
        env_kernel(
            block, unit, scale, env_from(ids), ids[2], grid_ref, other_ref, results[n_out], results[n_out + 1 :], env_spread
        )


def env_kernel(block, unit, scale, from_ref, own, left_ref, right_ref, keep_ref, send_refs, spread):
    ratio = 4 * block // LANES
    pairs = block * ratio // (2 * unit)
    per = send_refs[0].shape[0]
    for m in range(4):
        left = left_ref[pl.ds(pl.multiple_of(from_ref[m] * block, block), block), :]
        value = lax.dot_general(left, right_ref[...], (((1,), (1,)), ((), ())), preferred_element_type=jnp.float32)
        for c in range(ratio):
            spread[pl.ds(c, block, stride=ratio), :] = value[:, c * LANES : (c + 1) * LANES] * scale
        for g in range(pairs):
            to = (m * pairs + g) * unit
            keep_ref[to : to + unit, :] = spread[pl.ds(pl.multiple_of((2 * g + own) * unit, unit), unit), :]
            away = spread[pl.ds(pl.multiple_of((2 * g + 1 - own) * unit, unit), unit), :].astype(jnp.bfloat16)
            step = min(unit, per)
            for k in range(0, unit, step):
                at = to + k
                send_refs[at // per][at % per : at % per + step, :] = away[k : k + step, :]


def apply_gate(ids, gate_matrix, states, in_place, out_place, width, linear, sizes, after, env=None, work=0):
    gate = gate_matrix.shape[0]
    block = gate // 4
    rows = block * width // LANES
    shapes = [jax.ShapeDtypeStruct((rows, LANES), jnp.bfloat16)] * 4
    if sizes is not None:
        shapes = [jax.ShapeDtypeStruct((size, width), jnp.bfloat16) for size in sizes]
    n_out = len(shapes)
    arrays = [*states, gate_matrix]
    whole = pltpu.VMEM((gate, width), jnp.bfloat16)
    scratch = [pltpu.VMEM((rows, LANES), jnp.float32)]
    if env is None:
        shapes.append(jax.ShapeDtypeStruct((gate, width), jnp.bfloat16))
        scratch = [pltpu.VMEM((8, LANES), jnp.bfloat16)] + scratch
        numbers = None
    else:
        other, *numbers = env
        lines = gate * gate // (2 * LANES)
        shapes.append(jax.ShapeDtypeStruct((lines, LANES), jnp.float32))
        shapes += [jax.ShapeDtypeStruct((lines // ENV_CUTS, LANES), jnp.bfloat16)] * ENV_CUTS
        arrays = [*states, other, gate_matrix]
        scratch = [whole] + scratch + [whole, pltpu.VMEM((block * gate // LANES, LANES), jnp.float32)]
    kernel = functools.partial(gate_kernel, block, linear, sizes, numbers, in_place, out_place)
    got, token = call(kernel, shapes, ids, arrays, after, scratch, work=work)
    return got[:n_out], got[n_out:], token


def fold(ids, base, incoming, left, group, unit, after, work=0):
    lead = [bit for bit in left if bit not in group]
    stride = {bit: unit << (len(left) - 1 - n) for n, bit in enumerate(left)}
    flips = [sum(((k >> n) & 1) << bit for n, bit in enumerate(group)) for k in range(2 ** len(group))]
    rows = unit << len(lead)

    arrays = [piece for one in incoming for piece in one]

    def kernel(ids, ins, outs):
        def summed(at):
            value = ins[0][at, :]
            count = 1
            for one in incoming:
                per = one[0].shape[0]
                start = at.start
                inside = pl.ds(start - start // per * per if len(one) > 1 else start, unit)
                inside = pl.ds(pl.multiple_of(inside.start, unit), unit) if group else inside
                part = ins[count][inside, :].astype(jnp.float32)
                for k in range(1, len(one)):
                    part = jnp.where(start // per == k, ins[count + k][inside, :].astype(jnp.float32), part)
                value = value + part
                count += len(one)
            return value

        for n in sorted(range(len(flips)), key=lambda n: n == 0):
            origin = sum((((ids[3] ^ flips[n]) >> bit) & 1) * stride[bit] for bit in group)
            for k in range(2 ** len(lead)):
                shift = sum(((k >> (len(lead) - 1 - i)) & 1) * stride[bit] for i, bit in enumerate(lead))
                at = pl.ds(pl.multiple_of(origin + shift, unit), unit) if group else pl.ds(shift, unit)
                outs[n][k * unit : (k + 1) * unit, :] = summed(at).astype(outs[n].dtype)

    shapes = [jax.ShapeDtypeStruct((rows, LANES), jnp.float32 if flip == 0 else jnp.bfloat16) for flip in flips]
    (own, *pieces), token = call(kernel, shapes, ids, [base, *arrays], after, work=work)
    return own, pieces, flips[1:], token


def on_device(forward_state, adjoint_state, gate_matrix):
    row_count, col_count = lax.axis_size("row"), lax.axis_size("col")
    row_bits, col_bits = row_count.bit_length() - 1, col_count.bit_length() - 1
    me = lax.axis_index("row") * col_count + lax.axis_index("col")
    top, side = col_bits - 1, col_bits
    p, q, e = (me >> side) & 1, (me >> top) & 1, me & 1
    gate = gate_matrix.shape[0]
    local = forward_state.shape[0]
    width = local // gate
    scale = 1.0 / math.sqrt(row_count * col_count * local / gate)
    unit = gate * gate // (row_count * col_count * LANES)
    half = gate // 2
    ids = jnp.stack([p, q, e, me]).astype(jnp.int32)

    def across_x(value):
        return sent(value, lambda i: i ^ (1 << side))

    def across_z(value):
        return sent(value, lambda i: i ^ (1 << top))

    def across_core(value):
        return sent(value, lambda i: i ^ 1)

    def home(value, flip):
        return sent(value, lambda i: (i ^ ((i & 1) << top)) ^ flip)

    forward = forward_state.reshape(-1, LANES)
    adjoint = adjoint_state.reshape(-1, LANES)
    quarter = forward.shape[0] // 4

    def quarter_of(state, i, j):
        return lax.dynamic_slice_in_dim(state, ((p ^ i) * 2 + (q ^ j)) * quarter, quarter, 0)

    flight = {}
    chain = []

    def gates(name):
        waits = [value for key in KNOBS.get("waits", {}).get(name, ()) for value in flight[key]]
        before = chain[-1:]
        if not waits:
            return before
        free = name in KNOBS.get("free", ())
        token = arrived(ids, waits, [] if free else before, work=KNOBS.get("lead", {}).get(name, 0))
        return [token, *before] if free else [token]

    def link(token):
        chain.append(token)

    def work(name):
        return KNOBS.get("work", {}).get(name, 0)

    flight["Z1"] = [across_z(quarter_of(forward, 0, 1))]
    flight["X1"] = [across_x(quarter_of(forward, 1, 1))]
    flight["Z2"] = [across_z(flight["X1"][0])]
    (f_own, f_beside, a_relay), token = take(
        ids, [[(forward, 0, 0)], [(forward, 1, 0)], [(adjoint, 1, 1)]], [arrived(ids, flight["X1"]), *gates("take1")]
    )
    link(token)
    flight["X2"] = [across_x(f_beside)]
    flight["X3"] = [across_x(a_relay)]
    (a_own, a_beside, *a_over), token = take(
        ids,
        [[(adjoint, 0, 0)], [(adjoint, 1, 0)]]
        + (
            [[(adjoint, 0, 1), flight["X3"][0]]]
            if KNOBS.get("join_in", True)
            else [[(adjoint, 0, 1)], [flight["X3"][0]]]
        ),
        gates("take2"),
    )
    link(token)
    flight["Z3"] = [across_z(one) for one in a_over]
    flight["X4"] = [across_x(a_beside)]
    forward_in = [f_own, *flight["Z1"], *flight["X2"], *flight["Z2"]]
    adjoint_in = [a_own, *flight["Z3"], *flight["X4"]]

    def forward_place(ids):
        return [quarter_at(ids, i, j) for i in range(2) for j in range(2)]

    def adjoint_place(ids):
        return [quarter_at(ids, *at) for at in ((0, 0), (0, 1), (1, 1), (1, 0))]

    def first_out(ids):
        kept = ids[1] ^ ids[2]
        return [kept, 2 + kept, 1 - kept, 3 - kept]

    def first_from(ids):
        kept = ids[1] ^ ids[2]
        return [2 * kept, 2 * (1 - kept), 1 + 2 * kept, 1 + 2 * (1 - kept)]

    def second_in(ids):
        return [ids[2], 2 + ids[2], 1 - ids[2], 3 - ids[2]]

    def second_out(ids):
        return [(ids[0] ^ i) * 2 + (ids[2] ^ j) for i in range(2) for j in range(2)]

    def first_gate(name, blocks, place, env=None):
        sizes = [half] + [half // CORE_CUTS] * CORE_CUTS
        (keep, *send), extra, token = apply_gate(
            ids, gate_matrix, blocks, place, first_out, width, True, sizes, gates(name), env, work(name)
        )
        link(token)
        return [keep] + [across_core(one) for one in send], extra

    def second_gate(name, blocks, env=None):
        out, extra, token = apply_gate(
            ids, gate_matrix, blocks, second_in, second_out, width, False, None, gates(name), env, work(name)
        )
        link(token)
        return out, extra

    def final_place(ids, i, flip):
        return (ids[0] ^ i) * 2 + (ids[1] ^ ids[2] ^ flip)

    def by_row(ids):
        return [final_place(ids, i, flip) for i in range(2) for flip in range(2)]

    def by_flip(ids):
        return [final_place(ids, i, flip) for flip in range(2) for i in range(2)]

    def leave(name, out):
        style = KNOBS.get("out_" + name, "direct")
        flight[name + "_X"] = [across_x(one) for one in out[2:]]
        if style == "packed":
            packed, token = pack(ids, [[out[k], flight[name + "_X"][k]] for k in range(2)], gates(name + "_pack"))
            link(token)
            flight[name + "_near"] = flight[name + "_far"] = [home(one, flip) for flip, one in enumerate(packed)]
            return
        near = out[:2]
        if style == "gated":
            near, token = pack(ids, [[one] for one in near], gates(name + "_pack"))
            link(token)
        flight[name + "_near"] = [home(one, flip) for flip, one in enumerate(near)]
        far = flight[name + "_X"]
        if KNOBS.get("far_" + name, False):
            far, token = pack(ids, [[one] for one in far], gates(name + "_far_pack"))
            link(token)
        flight[name + "_far"] = [home(one, flip) for flip, one in enumerate(far)]

    def finish(name):
        if KNOBS.get("out_" + name, "direct") == "packed":
            pieces, places = flight[name + "_near"], by_flip
        else:
            pieces, places = flight[name + "_near"] + flight[name + "_far"], by_row
        (whole,), token = put(ids, pieces, places, gates("put_" + name))
        link(token)
        return whole.reshape(-1)

    upper, middle = list(range(side + 1, side + row_bits)), list(range(1, top))
    last = [[bit] for bit in middle[1:]] + [[top], []]
    orders = {
        "y_xz": [upper, [side] + middle[:1]],
        "y_x_z": [upper, [side], middle[:1]],
        "x_yz": [[side], upper + middle[:1]],
        "yx_z": [upper + [side], middle[:1]],
        "yxz": [upper + [side] + middle[:1]],
        "y_z_x": [upper, middle[:1], [side]],
    }
    order = {k: orders[KNOBS.get("order" + k, "y_xz")] + last for k in "12"}
    sums = {}

    def begin(key, extra):
        keep, *send = extra
        left = sorted((bit for group in order[key] for bit in group), reverse=True)
        sums[key] = keep, [[across_core(one) for one in send]], left, 0

    def step(key):
        base, incoming, left, n = sums[key]
        name = "F%s_%d" % (key, n)
        group = order[key][n]
        own, pieces, flips, token = fold(ids, base, incoming, left, group, unit, gates(name), work(name))
        link(token)
        come = [[sent(one, lambda i, flip=flip: i ^ flip)] for one, flip in zip(pieces, flips, strict=True)]
        flight[name] = [one for (one,) in come]
        sums[key] = own, come, [bit for bit in left if bit not in group], n + 1

    def steps_left(key):
        return len(order[key]) - sums[key][3]

    results = {}
    f_mid, (f_start,) = first_gate("G1f", forward_in, forward_place)
    f_out, (f_moved,) = second_gate("G2f", f_mid)
    leave("f", f_out)
    a_mid, extra = first_gate("GE1", adjoint_in, adjoint_place, (f_start, first_from, unit, scale))
    begin("1", extra)
    for name in KNOBS.get("plan", "1G21f122a12"):
        if name == "G":
            a_out, extra = second_gate("GE2", a_mid, (f_moved, second_out, unit, scale))
            begin("2", extra)
            leave("a", a_out)
        elif name in sums:
            if steps_left(name) > 1:
                step(name)
        else:
            results[name] = finish(name)
    for key in "12":
        while steps_left(key):
            step(key)
    return results["f"], results["a"], sums["1"][0].reshape(-1), sums["2"][0].reshape(-1)


def solution(mesh):
    in_specs = (P(AXES), P(AXES), P())
    out_specs = (P(AXES),) * 4
    return jax.shard_map(on_device, mesh=mesh, in_specs=in_specs, out_specs=out_specs, check_vma=False)
```

```python
import functools
import math

import jax
import jax.numpy as jnp
from jax import lax
from jax.experimental import pallas as pl
from jax.experimental.pallas import tpu as pltpu
from jax.sharding import PartitionSpec as P

AXES = ("row", "col")
LANES = 128
KNOBS = {'out_f': 'packed', 'out_a': 'packed', 'plan': '1G2p12fJaE', 'free': ['take2', 'F2_0', 'GE2', 'F12_2'], 'cuts': {'G1f': 4}, 'order': 'y,xz,z', 'waits': {'take2': ['Z1', 'Z2'], 'f_pack': ['Z3', 'f_X'], 'F2_0': ['f_near'], 'GE2': ['f_X']}, 'lead': {'take2': 20000000000, 'F2_0': 20000000000, 'GE2': 20000000000, 'F12_2': 20000000000}}


SMEM = pl.BlockSpec(memory_space=pltpu.SMEM)
VMEM = pl.BlockSpec(memory_space=pltpu.VMEM)
HBM = pl.BlockSpec(memory_space=pltpu.HBM)
ANY = pl.BlockSpec(memory_space=pl.ANY)
VMEM_BYTES = 16 * 2**20
ENV_CUTS = 1


def sent(value, target):
    count = lax.axis_size("row") * lax.axis_size("col")
    return lax.ppermute(value, AXES, [(i, target(i)) for i in range(count)])

TOKEN = jax.ShapeDtypeStruct((8, LANES), jnp.float32)


def call(kernel, shapes, ids, arrays, after=(), scratch=(), raw_in=(), raw_out=(), work=0):
    n_in, n_out, n_after = len(arrays), len(shapes), len(after)

    def body(ids_ref, *refs):
        ins, refs = refs[:n_in], refs[n_in + n_after :]
        kernel([ids_ref[k] for k in range(4)], ins, refs[:n_out], *refs[n_out + 1 :])

    *results, token = pl.pallas_call(
        body,
        out_shape=[*shapes, TOKEN],
        in_specs=[SMEM] + [HBM if k in raw_in else VMEM for k in range(n_in)] + [ANY] * n_after,
        out_specs=[HBM if k in raw_out else VMEM for k in range(n_out)] + [ANY],
        scratch_shapes=list(scratch),
        compiler_params=pltpu.CompilerParams(vmem_limit_bytes=VMEM_BYTES),
        cost_estimate=pl.CostEstimate(flops=work, bytes_accessed=0, transcendentals=0),
    )(ids, *arrays, *after)
    return results, token


def arrived(ids, values, after=(), work=0):
    return call(lambda ids, ins, outs: None, [], ids, [], [*values, *after], work=work)[1]


def quarter_at(ids, i, j):
    return (ids[0] ^ i) * 2 + (ids[1] ^ j)


def take(ids, wanted, after=()):
    states = []
    for pieces in wanted:
        for one in pieces:
            if isinstance(one, tuple) and not any(one[0] is state for state in states):
                states.append(one[0])
    rows = states[0].shape[0] // 4
    arrays = [one for pieces in wanted for one in pieces if not isinstance(one, tuple)]
    plan = []
    for k, pieces in enumerate(wanted):
        for n, one in enumerate(pieces):
            if isinstance(one, tuple):
                plan.append((k, n, next(i for i, state in enumerate(states) if state is one[0]), one[1:]))
            else:
                plan.append((k, n, next(i for i, other in enumerate(arrays) if other is one), None))
    count = sum(at is not None for *_, at in plan)

    def kernel(ids, ins, outs, sems):
        copies = []
        for k, n, i, at in plan:
            if at is not None:
                start = pl.multiple_of(quarter_at(ids, *at) * rows, rows)
                target = outs[k].at[pl.ds(n * rows, rows)]
                copies.append(pltpu.make_async_copy(ins[i].at[pl.ds(start, rows)], target, sems.at[len(copies)]))
                copies[-1].start()
        for k, n, i, at in plan:
            if at is None:
                outs[k][n * rows : (n + 1) * rows, :] = ins[len(states) + i][...]
        for copy in copies:
            copy.wait()

    shapes = [jax.ShapeDtypeStruct((rows * len(pieces), LANES), states[0].dtype) for pieces in wanted]
    scratch = [pltpu.SemaphoreType.DMA((count,))]
    return call(kernel, shapes, ids, states + arrays, after, scratch, raw_in=range(len(states)))


def put(ids, pieces, places, after):
    count = 4
    rows = sum(piece.shape[0] for piece in pieces) // count

    def kernel(ids, ins, outs, sems):
        copies, at = [], places(ids)
        for piece in ins:
            for k in range(0, piece.shape[0], rows):
                start = pl.multiple_of(at[len(copies)] * rows, rows)
                target = outs[0].at[pl.ds(start, rows)]
                copies.append(pltpu.make_async_copy(piece.at[pl.ds(k, rows)], target, sems.at[len(copies)]))
                copies[-1].start()
        for copy in copies:
            copy.wait()

    shapes = [jax.ShapeDtypeStruct((rows * count, LANES), pieces[0].dtype)]
    scratch = [pltpu.SemaphoreType.DMA((count,))]
    return call(kernel, shapes, ids, pieces, after, scratch, raw_out=[0])


def pack(ids, rows, arrays, groups, after):
    def kernel(ids, ins, outs):
        for group, out in zip(groups, outs, strict=True):
            for n, (k, at) in enumerate(group):
                out[n * rows : (n + 1) * rows, :] = ins[k][at * rows : (at + 1) * rows, :]

    shapes = [jax.ShapeDtypeStruct((len(group) * rows, LANES), arrays[0].dtype) for group in groups]
    return call(kernel, shapes, ids, arrays, after)


def load_state(block, linear, states, place_ref, moved_ref, spread):
    ratio = moved_ref.shape[1] // LANES
    if linear:
        lines, n = block * ratio, 0
        for state in states:
            for k in range(0, state.shape[0], lines):
                rows = pl.ds(pl.multiple_of(place_ref[n] * block, block), block)
                spread[...] = state[k : k + lines, :].astype(jnp.float32)
                for c in range(ratio):
                    part = spread[pl.ds(c, block, stride=ratio), :]
                    moved_ref[rows, c * LANES : (c + 1) * LANES] = part.astype(jnp.bfloat16)
                n += 1
        return
    row = 0
    for state in states:
        step = min(block, state.shape[0])
        for k in range(0, state.shape[0], step):
            start = pl.multiple_of(place_ref[row // block] * block + row % block, step)
            moved_ref[pl.ds(start, step), :] = state[k : k + step, :]
            row += step


def gate_kernel(block, linear, sizes, env, in_place, out_place, ids, ins, results, moved_ref, *refs):
    in_ref, out_ref = in_place(ids), out_place(ids)
    n_out = (4 if env is None else 3) if sizes is None else len(sizes)
    outs = results[:n_out]
    spread = refs[0]
    if env is None:
        *states, gate_ref = ins
        moved_ref = results[n_out]
    else:
        *states, other_ref, gate_ref = ins
        grid_ref, env_spread = refs[1], refs[2]
    ratio = moved_ref.shape[1] // LANES
    load_state(block, linear, states, in_ref, moved_ref, spread)
    for m in range(4):
        rows = pl.ds(pl.multiple_of(out_ref[m] * block, block), block)
        total = jnp.dot(gate_ref[rows, :], moved_ref[...], preferred_element_type=jnp.float32)
        rounded = total.astype(jnp.bfloat16)
        if env is not None:
            grid_ref[m * block : (m + 1) * block, :] = rounded
        if sizes is None:
            for c in range(ratio):
                spread[pl.ds(c, block, stride=ratio), :] = total[:, c * LANES : (c + 1) * LANES]
            out, lines = outs[min(m, n_out - 1)], spread.shape[0]
            row = lines if m >= n_out else 0
            out[row : row + lines, :] = spread[...].astype(jnp.bfloat16)
            continue
        row = 0
        for out in outs:
            first, last = max(row, m * block), min(row + out.shape[0], (m + 1) * block)
            if first < last:
                out[first - row : last - row, :] = rounded[first - m * block : last - m * block, :]
            row += out.shape[0]
    if env is not None:
        env_from, unit, scale = env
        env_kernel(
            block, unit, scale, env_from(ids), ids[2], grid_ref, other_ref, results[n_out], results[n_out + 1 :], env_spread
        )


def env_kernel(block, unit, scale, from_ref, own, left_ref, right_ref, keep_ref, send_refs, spread):
    ratio = 4 * block // LANES
    pairs = block * ratio // (2 * unit)
    per = send_refs[0].shape[0]
    for m in range(4):
        left = left_ref[pl.ds(pl.multiple_of(from_ref[m] * block, block), block), :]
        value = lax.dot_general(left, right_ref[...], (((1,), (1,)), ((), ())), preferred_element_type=jnp.float32)
        for c in range(ratio):
            spread[pl.ds(c, block, stride=ratio), :] = value[:, c * LANES : (c + 1) * LANES] * scale
        for g in range(pairs):
            to = (m * pairs + g) * unit
            keep_ref[to : to + unit, :] = spread[pl.ds(pl.multiple_of((2 * g + own) * unit, unit), unit), :]
            away = spread[pl.ds(pl.multiple_of((2 * g + 1 - own) * unit, unit), unit), :].astype(jnp.bfloat16)
            step = min(unit, per)
            for k in range(0, unit, step):
                at = to + k
                send_refs[at // per][at % per : at % per + step, :] = away[k : k + step, :]


def apply_gate(ids, gate_matrix, states, in_place, out_place, width, linear, sizes, after, env=None, work=0):
    gate = gate_matrix.shape[0]
    block = gate // 4
    rows = block * width // LANES
    shapes = [jax.ShapeDtypeStruct((rows, LANES), jnp.bfloat16)] * 4
    if sizes is None and env is not None:
        shapes = shapes[:2] + [jax.ShapeDtypeStruct((2 * rows, LANES), jnp.bfloat16)]
    if sizes is not None:
        shapes = [jax.ShapeDtypeStruct((size, width), jnp.bfloat16) for size in sizes]
    n_out = len(shapes)
    arrays = [*states, gate_matrix]
    whole = pltpu.VMEM((gate, width), jnp.bfloat16)
    scratch = [pltpu.VMEM((rows, LANES), jnp.float32)]
    if env is None:
        shapes.append(jax.ShapeDtypeStruct((gate, width), jnp.bfloat16))
        scratch = [pltpu.VMEM((8, LANES), jnp.bfloat16)] + scratch
        numbers = None
    else:
        other, *numbers = env
        lines = gate * gate // (2 * LANES)
        shapes.append(jax.ShapeDtypeStruct((lines, LANES), jnp.float32))
        shapes += [jax.ShapeDtypeStruct((lines // ENV_CUTS, LANES), jnp.bfloat16)] * ENV_CUTS
        arrays = [*states, other, gate_matrix]
        scratch = [whole] + scratch + [whole, pltpu.VMEM((block * gate // LANES, LANES), jnp.float32)]
    kernel = functools.partial(gate_kernel, block, linear, sizes, numbers, in_place, out_place)
    got, token = call(kernel, shapes, ids, arrays, after, scratch, work=work)
    return got[:n_out], got[n_out:], token


def fold(ids, sums, count, left, group, unit, after, work=0):
    lead = [bit for bit in left if bit not in group]
    stride = {bit: unit << (len(left) - 1 - n) for n, bit in enumerate(left)}
    flips = [sum(((k >> n) & 1) << bit for n, bit in enumerate(group)) for k in range(2 ** len(group))]
    rows = unit << len(lead)
    arrays = [one for base, incoming in sums for one in [base, *incoming]]

    def kernel(ids, ins, outs):
        for flip, out in sorted(zip(flips, outs, strict=True), key=lambda one: one[0] == 0):
            origin = sum((((ids[3] ^ flip) >> bit) & 1) * stride[bit] for bit in group)
            refs = list(ins)
            for n in range(len(sums) * count):
                if n % count == 0:
                    mine, refs = refs[: 1 + len(sums[n // count][1])], refs[1 + len(sums[n // count][1]) :]
                first = n % count * (unit << len(left))
                for k in range(2 ** len(lead)):
                    shift = sum(((k >> (len(lead) - 1 - i)) & 1) * stride[bit] for i, bit in enumerate(lead))
                    at = pl.ds(pl.multiple_of(first + origin + shift, unit), unit)
                    value = mine[0][at, :]
                    for one in mine[1:]:
                        value = value + one[at, :].astype(jnp.float32)
                    out[n * rows + k * unit : n * rows + (k + 1) * unit, :] = value.astype(out.dtype)

    shapes = [
        jax.ShapeDtypeStruct((len(sums) * count * rows, LANES), jnp.float32 if flip == 0 else jnp.bfloat16) for flip in flips
    ]
    (own, *pieces), token = call(kernel, shapes, ids, arrays, after, work=work)
    return own, pieces, flips[1:], token


def add_up(ids, base, incoming, count, after):
    rows = base.shape[0] // count

    def kernel(ids, ins, outs):
        for n, out in enumerate(outs):
            value = ins[0][n * rows : (n + 1) * rows, :]
            for one in ins[1:]:
                value = value + one[n * rows : (n + 1) * rows, :].astype(jnp.float32)
            out[...] = value

    shapes = [jax.ShapeDtypeStruct((rows, LANES), base.dtype)] * count
    return call(kernel, shapes, ids, [base, *incoming], after)


def on_device(forward_state, adjoint_state, gate_matrix):
    row_count, col_count = lax.axis_size("row"), lax.axis_size("col")
    row_bits, col_bits = row_count.bit_length() - 1, col_count.bit_length() - 1
    me = lax.axis_index("row") * col_count + lax.axis_index("col")
    top, side = col_bits - 1, col_bits
    p, q, e = (me >> side) & 1, (me >> top) & 1, me & 1
    gate = gate_matrix.shape[0]
    local = forward_state.shape[0]
    width = local // gate
    scale = 1.0 / math.sqrt(row_count * col_count * local / gate)
    unit = gate * gate // (row_count * col_count * LANES)
    half = gate // 2
    ids = jnp.stack([p, q, e, me]).astype(jnp.int32)

    def across_x(value):
        return sent(value, lambda i: i ^ (1 << side))

    def across_z(value):
        return sent(value, lambda i: i ^ (1 << top))

    def across_core(value):
        return sent(value, lambda i: i ^ 1)

    def home(value, flip):
        return sent(value, lambda i: (i ^ ((i & 1) << top)) ^ flip)

    forward = forward_state.reshape(-1, LANES)
    adjoint = adjoint_state.reshape(-1, LANES)
    quarter = forward.shape[0] // 4

    def quarter_of(state, i, j):
        return lax.dynamic_slice_in_dim(state, ((p ^ i) * 2 + (q ^ j)) * quarter, quarter, 0)

    flight = {}
    chain = []

    def gates(name):
        waits = [value for key in KNOBS.get("waits", {}).get(name, ()) for value in flight[key]]
        before = chain[-1:]
        if not waits:
            return before
        free = name in KNOBS.get("free", ())
        token = arrived(ids, waits, [] if free else before, work=KNOBS.get("lead", {}).get(name, 0))
        return [token, *before] if free else [token]

    def link(token):
        chain.append(token)

    def work(name):
        return KNOBS.get("work", {}).get(name, 0)

    flight["Z1"] = [across_z(quarter_of(forward, 0, 1))]
    flight["X1"] = [across_x(quarter_of(forward, 1, 1))]
    flight["Z2"] = [across_z(flight["X1"][0])]
    (f_own, f_beside, a_relay), token = take(
        ids, [[(forward, 0, 0)], [(forward, 1, 0)], [(adjoint, 1, 1)]], [arrived(ids, flight["X1"]), *gates("take1")]
    )
    link(token)
    flight["X2"] = [across_x(f_beside)]
    flight["X3"] = [across_x(a_relay)]
    (a_own, a_beside, *a_over), token = take(
        ids,
        [[(adjoint, 0, 0)], [(adjoint, 1, 0)]]
        + (
            [[(adjoint, 0, 1), flight["X3"][0]]]
            if KNOBS.get("join_in", True)
            else [[(adjoint, 0, 1)], [flight["X3"][0]]]
        ),
        gates("take2"),
    )
    link(token)
    flight["Z3"] = [across_z(one) for one in a_over]
    flight["X4"] = [across_x(a_beside)]
    forward_in = [f_own, *flight["Z1"], *flight["X2"], *flight["Z2"]]
    adjoint_in = [a_own, *flight["Z3"], *flight["X4"]]

    def forward_place(ids):
        return [quarter_at(ids, i, j) for i in range(2) for j in range(2)]

    def adjoint_place(ids):
        return [quarter_at(ids, *at) for at in ((0, 0), (0, 1), (1, 1), (1, 0))]

    def first_out(ids):
        kept = ids[1] ^ ids[2]
        return [kept, 2 + kept, 1 - kept, 3 - kept]

    def first_from(ids):
        kept = ids[1] ^ ids[2]
        return [2 * kept, 2 * (1 - kept), 1 + 2 * kept, 1 + 2 * (1 - kept)]

    def second_in(ids):
        return [ids[2], 2 + ids[2], 1 - ids[2], 3 - ids[2]]

    def second_out(ids):
        return [(ids[0] ^ i) * 2 + (ids[2] ^ j) for i in range(2) for j in range(2)]

    def first_gate(name, blocks, place, env=None):
        cuts = KNOBS.get("cuts", {}).get(name, 1)
        sizes = [half] + [half // cuts] * cuts
        (keep, *send), extra, token = apply_gate(
            ids, gate_matrix, blocks, place, first_out, width, True, sizes, gates(name), env, work(name)
        )
        link(token)
        return [keep] + [across_core(one) for one in send], extra

    def second_gate(name, blocks, env=None):
        out, extra, token = apply_gate(
            ids, gate_matrix, blocks, second_in, second_out, width, False, None, gates(name), env, work(name)
        )
        link(token)
        return out, extra

    def final_place(ids, i, flip):
        return (ids[0] ^ i) * 2 + (ids[1] ^ ids[2] ^ flip)

    def by_row(ids):
        return [final_place(ids, i, flip) for i in range(2) for flip in range(2)]

    def by_flip(ids):
        return [final_place(ids, i, flip) for flip in range(2) for i in range(2)]

    def cross(name, out):
        flight[name + "_X"] = [across_x(one) for one in out[2:]]

    def leave(name, out):
        style = KNOBS.get("out_" + name, "direct")
        if style == "packed":
            joined = len(out) == 3
            groups = [[(k, 0), (2, k) if joined else (2 + k, 0)] for k in range(2)]
            packed, token = pack(ids, quarter, [*out[:2], *flight[name + "_X"]], groups, gates(name + "_pack"))
            link(token)
            flight[name + "_near"] = flight[name + "_far"] = [home(one, flip) for flip, one in enumerate(packed)]
            return
        near = out[:2]
        if style == "gated":
            near, token = pack(ids, quarter, near, [[(0, 0)], [(1, 0)]], gates(name + "_pack"))
            link(token)
        flight[name + "_near"] = [home(one, flip) for flip, one in enumerate(near)]
        far = flight[name + "_X"]
        if KNOBS.get("far_" + name, False):
            far, token = pack(ids, quarter, far, [[(0, 0)], [(1, 0)]], gates(name + "_far_pack"))
            link(token)
        flight[name + "_far"] = [home(one, flip) for flip, one in enumerate(far)]

    def finish(name):
        if KNOBS.get("out_" + name, "direct") == "packed":
            pieces, places = flight[name + "_near"], by_flip
        else:
            pieces, places = flight[name + "_near"] + flight[name + "_far"], by_row
        (whole,), token = put(ids, pieces, places, gates("put_" + name))
        link(token)
        return whole.reshape(-1)

    upper, middle = list(range(side + 1, side + row_bits)), list(range(1, top))
    singles = [[bit] for bit in middle[1:]]
    order = {
        "y,x,zz": [upper, [side], *singles, middle[:1] + [top]],
        "y,x,z,z": [upper, [side], *singles, middle[:1], [top]],
        "y,xz,z": [upper, [side] + middle[:1], *singles, [top]],
        "y,z,xz": [upper, middle[:1], *singles, [side, top]],
        "yx,zz": [upper + [side], *singles, middle[:1] + [top]],
        "yx,z,z": [upper + [side], *singles, middle[:1], [top]],
        "y,xzz": [upper, *singles, [side] + middle[:1] + [top]],
    }[KNOBS.get("order", "y,x,zz")]
    everything = sorted((bit for group in order for bit in group), reverse=True)
    sums = {}

    def begin(key, extra):
        keep, *send = extra
        sums[key] = keep, [across_core(one) for one in send], everything, 0

    def step(keys):
        known = [keys] if keys in sums else list(keys)
        _, _, left, n = sums[known[0]]
        name = "F%s_%d" % (keys, n)
        group = order[n]
        parts = [sums[key][:2] for key in known]
        own, pieces, flips, token = fold(ids, parts, len(keys) // len(known), left, group, unit, gates(name), work(name))
        link(token)
        come = [sent(one, lambda i, flip=flip: i ^ flip) for one, flip in zip(pieces, flips, strict=True)]
        flight[name] = come
        sums[keys] = own, come, [bit for bit in left if bit not in group], n + 1

    results = {}
    f_mid, (f_start,) = first_gate("G1f", forward_in, forward_place)
    f_out, (f_moved,) = second_gate("G2f", f_mid)
    cross("f", f_out)
    leave("f", f_out)
    a_mid, extra = first_gate("GE1", adjoint_in, adjoint_place, (f_start, first_from, unit, scale))
    begin("1", extra)
    for name in KNOBS["plan"]:
        if name == "G":
            a_out, extra = second_gate("GE2", a_mid, (f_moved, second_out, unit, scale))
            begin("2", extra)
            cross("a", a_out)
        elif name == "p":
            leave("a", a_out)
        elif name in "12":
            step(name)
        elif name == "J":
            while "12" not in sums and sums["2"][3] < len(order) - 1:
                step("1")
                step("2")
            step("12")
        elif name == "E":
            (env_one, env_two), token = add_up(ids, *sums["12"][:2], 2, gates("end"))
            link(token)
        else:
            results[name] = finish(name)
    return results["f"], results["a"], env_one.reshape(-1), env_two.reshape(-1)


def solution(mesh):
    in_specs = (P(AXES), P(AXES), P())
    out_specs = (P(AXES),) * 4
    return jax.shard_map(on_device, mesh=mesh, in_specs=in_specs, out_specs=out_specs, check_vma=False)
```

```python
import functools
import math

import jax
import jax.numpy as jnp
from jax import lax
from jax.experimental import pallas as pl
from jax.experimental.pallas import tpu as pltpu
from jax.sharding import PartitionSpec as P

AXES = ("row", "col")
LANES = 128
KNOBS = {'out_f': 'packed', 'out_a': 'packed', 'plan': '1G2p12JfaE', 'free': ['take2', 'F2_0', 'GE2', 'F12_2'], 'cuts': {'G1f': 4}, 'order': 'y,xz,z', 'waits': {'take2': ['Z1', 'Z2'], 'f_pack': ['Z3', 'f_X'], 'F2_0': ['f_near'], 'GE2': ['f_X']}, 'lead': {'take2': 20000000000, 'F2_0': 20000000000, 'GE2': 20000000000, 'F12_2': 20000000000}, 'direct': ['f_pack', 'take1']}


SMEM = pl.BlockSpec(memory_space=pltpu.SMEM)
VMEM = pl.BlockSpec(memory_space=pltpu.VMEM)
HBM = pl.BlockSpec(memory_space=pltpu.HBM)
ANY = pl.BlockSpec(memory_space=pl.ANY)
VMEM_BYTES = 16 * 2**20
ENV_CUTS = 1


def sent(value, target):
    count = lax.axis_size("row") * lax.axis_size("col")
    return lax.ppermute(value, AXES, [(i, target(i)) for i in range(count)])

TOKEN = jax.ShapeDtypeStruct((8, LANES), jnp.float32)


def call(kernel, shapes, ids, arrays, after=(), scratch=(), raw_in=(), raw_out=(), work=0):
    n_in, n_out, n_after = len(arrays), len(shapes), len(after)

    def body(ids_ref, *refs):
        ins, refs = refs[:n_in], refs[n_in + n_after :]
        kernel([ids_ref[k] for k in range(4)], ins, refs[:n_out], *refs[n_out + 1 :])

    *results, token = pl.pallas_call(
        body,
        out_shape=[*shapes, TOKEN],
        in_specs=[SMEM] + [HBM if k in raw_in else VMEM for k in range(n_in)] + [ANY] * n_after,
        out_specs=[HBM if k in raw_out else VMEM for k in range(n_out)] + [ANY],
        scratch_shapes=list(scratch),
        compiler_params=pltpu.CompilerParams(vmem_limit_bytes=VMEM_BYTES),
        cost_estimate=pl.CostEstimate(flops=work, bytes_accessed=0, transcendentals=0),
    )(ids, *arrays, *after)
    return results, token


def arrived(ids, values, after=(), work=0):
    return call(lambda ids, ins, outs: None, [], ids, [], [*values, *after], work=work)[1]


def quarter_at(ids, i, j):
    return (ids[0] ^ i) * 2 + (ids[1] ^ j)


def take(ids, wanted, after=()):
    states = []
    for pieces in wanted:
        for one in pieces:
            if isinstance(one, tuple) and not any(one[0] is state for state in states):
                states.append(one[0])
    rows = states[0].shape[0] // 4
    arrays = [one for pieces in wanted for one in pieces if not isinstance(one, tuple)]
    plan = []
    for k, pieces in enumerate(wanted):
        for n, one in enumerate(pieces):
            if isinstance(one, tuple):
                plan.append((k, n, next(i for i, state in enumerate(states) if state is one[0]), one[1:]))
            else:
                plan.append((k, n, next(i for i, other in enumerate(arrays) if other is one), None))
    count = sum(at is not None for *_, at in plan)

    def kernel(ids, ins, outs, sems):
        copies = []
        for k, n, i, at in plan:
            if at is not None:
                start = pl.multiple_of(quarter_at(ids, *at) * rows, rows)
                target = outs[k].at[pl.ds(n * rows, rows)]
                copies.append(pltpu.make_async_copy(ins[i].at[pl.ds(start, rows)], target, sems.at[len(copies)]))
                copies[-1].start()
        for k, n, i, at in plan:
            if at is None:
                outs[k][n * rows : (n + 1) * rows, :] = ins[len(states) + i][...]
        for copy in copies:
            copy.wait()

    shapes = [jax.ShapeDtypeStruct((rows * len(pieces), LANES), states[0].dtype) for pieces in wanted]
    scratch = [pltpu.SemaphoreType.DMA((count,))]
    return call(kernel, shapes, ids, states + arrays, after, scratch, raw_in=range(len(states)))


def put(ids, pieces, places, after):
    count = 4
    rows = sum(piece.shape[0] for piece in pieces) // count

    def kernel(ids, ins, outs, sems):
        copies, at = [], places(ids)
        for piece in ins:
            for k in range(0, piece.shape[0], rows):
                start = pl.multiple_of(at[len(copies)] * rows, rows)
                target = outs[0].at[pl.ds(start, rows)]
                copies.append(pltpu.make_async_copy(piece.at[pl.ds(k, rows)], target, sems.at[len(copies)]))
                copies[-1].start()
        for copy in copies:
            copy.wait()

    shapes = [jax.ShapeDtypeStruct((rows * count, LANES), pieces[0].dtype)]
    scratch = [pltpu.SemaphoreType.DMA((count,))]
    return call(kernel, shapes, ids, pieces, after, scratch, raw_out=[0])


def pack(ids, rows, arrays, groups, after):
    def kernel(ids, ins, outs):
        for group, out in zip(groups, outs, strict=True):
            for n, (k, at) in enumerate(group):
                out[n * rows : (n + 1) * rows, :] = ins[k][at * rows : (at + 1) * rows, :]

    shapes = [jax.ShapeDtypeStruct((len(group) * rows, LANES), arrays[0].dtype) for group in groups]
    return call(kernel, shapes, ids, arrays, after)


def load_state(block, linear, states, place_ref, moved_ref, spread):
    ratio = moved_ref.shape[1] // LANES
    if linear:
        lines, n = block * ratio, 0
        for state in states:
            for k in range(0, state.shape[0], lines):
                rows = pl.ds(pl.multiple_of(place_ref[n] * block, block), block)
                spread[...] = state[k : k + lines, :].astype(jnp.float32)
                for c in range(ratio):
                    part = spread[pl.ds(c, block, stride=ratio), :]
                    moved_ref[rows, c * LANES : (c + 1) * LANES] = part.astype(jnp.bfloat16)
                n += 1
        return
    row = 0
    for state in states:
        step = min(block, state.shape[0])
        for k in range(0, state.shape[0], step):
            start = pl.multiple_of(place_ref[row // block] * block + row % block, step)
            moved_ref[pl.ds(start, step), :] = state[k : k + step, :]
            row += step


def gate_kernel(block, linear, sizes, env, in_place, out_place, ids, ins, results, moved_ref, *refs):
    in_ref, out_ref = in_place(ids), out_place(ids)
    n_out = (4 if env is None else 3) if sizes is None else len(sizes)
    outs = results[:n_out]
    spread = refs[0]
    if env is None:
        *states, gate_ref = ins
        moved_ref = results[n_out]
    else:
        *states, other_ref, gate_ref = ins
        grid_ref, env_spread = refs[1], refs[2]
    ratio = moved_ref.shape[1] // LANES
    load_state(block, linear, states, in_ref, moved_ref, spread)
    for m in range(4):
        rows = pl.ds(pl.multiple_of(out_ref[m] * block, block), block)
        total = jnp.dot(gate_ref[rows, :], moved_ref[...], preferred_element_type=jnp.float32)
        rounded = total.astype(jnp.bfloat16)
        if env is not None:
            grid_ref[m * block : (m + 1) * block, :] = rounded
        if sizes is None:
            for c in range(ratio):
                spread[pl.ds(c, block, stride=ratio), :] = total[:, c * LANES : (c + 1) * LANES]
            out, lines = outs[min(m, n_out - 1)], spread.shape[0]
            row = lines if m >= n_out else 0
            out[row : row + lines, :] = spread[...].astype(jnp.bfloat16)
            continue
        row = 0
        for out in outs:
            first, last = max(row, m * block), min(row + out.shape[0], (m + 1) * block)
            if first < last:
                out[first - row : last - row, :] = rounded[first - m * block : last - m * block, :]
            row += out.shape[0]
    if env is not None:
        env_from, unit, scale = env
        env_kernel(
            block, unit, scale, env_from(ids), ids[2], grid_ref, other_ref, results[n_out], results[n_out + 1 :], env_spread
        )


def env_kernel(block, unit, scale, from_ref, own, left_ref, right_ref, keep_ref, send_refs, spread):
    ratio = 4 * block // LANES
    pairs = block * ratio // (2 * unit)
    per = send_refs[0].shape[0]
    for m in range(4):
        left = left_ref[pl.ds(pl.multiple_of(from_ref[m] * block, block), block), :]
        value = lax.dot_general(left, right_ref[...], (((1,), (1,)), ((), ())), preferred_element_type=jnp.float32)
        for c in range(ratio):
            spread[pl.ds(c, block, stride=ratio), :] = value[:, c * LANES : (c + 1) * LANES] * scale
        for g in range(pairs):
            to = (m * pairs + g) * unit
            keep_ref[to : to + unit, :] = spread[pl.ds(pl.multiple_of((2 * g + own) * unit, unit), unit), :]
            away = spread[pl.ds(pl.multiple_of((2 * g + 1 - own) * unit, unit), unit), :].astype(jnp.bfloat16)
            step = min(unit, per)
            for k in range(0, unit, step):
                at = to + k
                send_refs[at // per][at % per : at % per + step, :] = away[k : k + step, :]


def apply_gate(ids, gate_matrix, states, in_place, out_place, width, linear, sizes, after, env=None, work=0):
    gate = gate_matrix.shape[0]
    block = gate // 4
    rows = block * width // LANES
    shapes = [jax.ShapeDtypeStruct((rows, LANES), jnp.bfloat16)] * 4
    if sizes is None and env is not None:
        shapes = shapes[:2] + [jax.ShapeDtypeStruct((2 * rows, LANES), jnp.bfloat16)]
    if sizes is not None:
        shapes = [jax.ShapeDtypeStruct((size, width), jnp.bfloat16) for size in sizes]
    n_out = len(shapes)
    arrays = [*states, gate_matrix]
    whole = pltpu.VMEM((gate, width), jnp.bfloat16)
    scratch = [pltpu.VMEM((rows, LANES), jnp.float32)]
    if env is None:
        shapes.append(jax.ShapeDtypeStruct((gate, width), jnp.bfloat16))
        scratch = [pltpu.VMEM((8, LANES), jnp.bfloat16)] + scratch
        numbers = None
    else:
        other, *numbers = env
        lines = gate * gate // (2 * LANES)
        shapes.append(jax.ShapeDtypeStruct((lines, LANES), jnp.float32))
        shapes += [jax.ShapeDtypeStruct((lines // ENV_CUTS, LANES), jnp.bfloat16)] * ENV_CUTS
        arrays = [*states, other, gate_matrix]
        scratch = [whole] + scratch + [whole, pltpu.VMEM((block * gate // LANES, LANES), jnp.float32)]
    kernel = functools.partial(gate_kernel, block, linear, sizes, numbers, in_place, out_place)
    got, token = call(kernel, shapes, ids, arrays, after, scratch, work=work)
    return got[:n_out], got[n_out:], token


def fold(ids, sums, count, left, group, unit, after, work=0):
    lead = [bit for bit in left if bit not in group]
    stride = {bit: unit << (len(left) - 1 - n) for n, bit in enumerate(left)}
    flips = [sum(((k >> n) & 1) << bit for n, bit in enumerate(group)) for k in range(2 ** len(group))]
    rows = unit << len(lead)
    arrays = [one for base, incoming in sums for one in [base, *incoming]]

    def kernel(ids, ins, outs):
        for flip, out in sorted(zip(flips, outs, strict=True), key=lambda one: one[0] == 0):
            origin = sum((((ids[3] ^ flip) >> bit) & 1) * stride[bit] for bit in group)
            refs = list(ins)
            for n in range(len(sums) * count):
                if n % count == 0:
                    mine, refs = refs[: 1 + len(sums[n // count][1])], refs[1 + len(sums[n // count][1]) :]
                first = n % count * (unit << len(left))
                for k in range(2 ** len(lead)):
                    shift = sum(((k >> (len(lead) - 1 - i)) & 1) * stride[bit] for i, bit in enumerate(lead))
                    at = pl.ds(pl.multiple_of(first + origin + shift, unit), unit)
                    value = mine[0][at, :]
                    for one in mine[1:]:
                        value = value + one[at, :].astype(jnp.float32)
                    out[n * rows + k * unit : n * rows + (k + 1) * unit, :] = value.astype(out.dtype)

    shapes = [
        jax.ShapeDtypeStruct((len(sums) * count * rows, LANES), jnp.float32 if flip == 0 else jnp.bfloat16) for flip in flips
    ]
    (own, *pieces), token = call(kernel, shapes, ids, arrays, after, work=work)
    return own, pieces, flips[1:], token


def add_up(ids, base, incoming, count, after):
    rows = base.shape[0] // count

    def kernel(ids, ins, outs):
        for n, out in enumerate(outs):
            value = ins[0][n * rows : (n + 1) * rows, :]
            for one in ins[1:]:
                value = value + one[n * rows : (n + 1) * rows, :].astype(jnp.float32)
            out[...] = value

    shapes = [jax.ShapeDtypeStruct((rows, LANES), base.dtype)] * count
    return call(kernel, shapes, ids, [base, *incoming], after)


def on_device(forward_state, adjoint_state, gate_matrix):
    row_count, col_count = lax.axis_size("row"), lax.axis_size("col")
    row_bits, col_bits = row_count.bit_length() - 1, col_count.bit_length() - 1
    me = lax.axis_index("row") * col_count + lax.axis_index("col")
    top, side = col_bits - 1, col_bits
    p, q, e = (me >> side) & 1, (me >> top) & 1, me & 1
    gate = gate_matrix.shape[0]
    local = forward_state.shape[0]
    width = local // gate
    scale = 1.0 / math.sqrt(row_count * col_count * local / gate)
    unit = gate * gate // (row_count * col_count * LANES)
    half = gate // 2
    ids = jnp.stack([p, q, e, me]).astype(jnp.int32)

    def across_x(value):
        return sent(value, lambda i: i ^ (1 << side))

    def across_z(value):
        return sent(value, lambda i: i ^ (1 << top))

    def across_core(value):
        return sent(value, lambda i: i ^ 1)

    def home(value, flip):
        return sent(value, lambda i: (i ^ ((i & 1) << top)) ^ flip)

    forward = forward_state.reshape(-1, LANES)
    adjoint = adjoint_state.reshape(-1, LANES)
    quarter = forward.shape[0] // 4

    def quarter_of(state, i, j):
        return lax.dynamic_slice_in_dim(state, ((p ^ i) * 2 + (q ^ j)) * quarter, quarter, 0)

    flight = {}
    chain = []

    def gates(name):
        waits = [value for key in KNOBS.get("waits", {}).get(name, ()) for value in flight[key]]
        before = chain[-1:]
        if not waits:
            return before
        if name in KNOBS.get("direct", ()):
            return [*waits, *before]
        free = name in KNOBS.get("free", ())
        token = arrived(ids, waits, [] if free else before, work=KNOBS.get("lead", {}).get(name, 0))
        return [token, *before] if free else [token]

    def link(token):
        chain.append(token)

    def work(name):
        return KNOBS.get("work", {}).get(name, 0)

    flight["Z1"] = [across_z(quarter_of(forward, 0, 1))]
    if KNOBS.get("take0", False):
        (through,), _ = take(ids, [[(forward, 1, 1)]])
    else:
        through = quarter_of(forward, 1, 1)
    flight["X1"] = [across_x(through)]
    flight["Z2"] = [across_z(flight["X1"][0])]
    (f_own, f_beside, a_relay), token = take(
        ids, [[(forward, 0, 0)], [(forward, 1, 0)], [(adjoint, 1, 1)]], [*(flight["X1"] if "take1" in KNOBS.get("direct", ()) else [arrived(ids, flight["X1"])]), *gates("take1")]
    )
    link(token)
    flight["X2"] = [across_x(f_beside)]
    flight["X3"] = [across_x(a_relay)]
    (a_own, a_beside, *a_over), token = take(
        ids,
        [[(adjoint, 0, 0)], [(adjoint, 1, 0)]]
        + (
            [[(adjoint, 0, 1), flight["X3"][0]]]
            if KNOBS.get("join_in", True)
            else [[(adjoint, 0, 1)], [flight["X3"][0]]]
        ),
        gates("take2"),
    )
    link(token)
    flight["Z3"] = [across_z(one) for one in a_over]
    flight["X4"] = [across_x(a_beside)]
    forward_in = [f_own, *flight["Z1"], *flight["X2"], *flight["Z2"]]
    adjoint_in = [a_own, *flight["Z3"], *flight["X4"]]

    def forward_place(ids):
        return [quarter_at(ids, i, j) for i in range(2) for j in range(2)]

    def adjoint_place(ids):
        return [quarter_at(ids, *at) for at in ((0, 0), (0, 1), (1, 1), (1, 0))]

    def first_out(ids):
        kept = ids[1] ^ ids[2]
        return [kept, 2 + kept, 1 - kept, 3 - kept]

    def first_from(ids):
        kept = ids[1] ^ ids[2]
        return [2 * kept, 2 * (1 - kept), 1 + 2 * kept, 1 + 2 * (1 - kept)]

    def second_in(ids):
        return [ids[2], 2 + ids[2], 1 - ids[2], 3 - ids[2]]

    def second_out(ids):
        return [(ids[0] ^ i) * 2 + (ids[2] ^ j) for i in range(2) for j in range(2)]

    def first_gate(name, blocks, place, env=None):
        cuts = KNOBS.get("cuts", {}).get(name, 1)
        sizes = [half] + [half // cuts] * cuts
        (keep, *send), extra, token = apply_gate(
            ids, gate_matrix, blocks, place, first_out, width, True, sizes, gates(name), env, work(name)
        )
        link(token)
        return [keep] + [across_core(one) for one in send], extra

    def second_gate(name, blocks, env=None):
        out, extra, token = apply_gate(
            ids, gate_matrix, blocks, second_in, second_out, width, False, None, gates(name), env, work(name)
        )
        link(token)
        return out, extra

    def final_place(ids, i, flip):
        return (ids[0] ^ i) * 2 + (ids[1] ^ ids[2] ^ flip)

    def by_row(ids):
        return [final_place(ids, i, flip) for i in range(2) for flip in range(2)]

    def by_flip(ids):
        return [final_place(ids, i, flip) for flip in range(2) for i in range(2)]

    def cross(name, out):
        flight[name + "_X"] = [across_x(one) for one in out[2:]]

    def leave(name, out):
        style = KNOBS.get("out_" + name, "direct")
        if style == "packed":
            joined = len(out) == 3
            groups = [[(k, 0), (2, k) if joined else (2 + k, 0)] for k in range(2)]
            packed, token = pack(ids, quarter, [*out[:2], *flight[name + "_X"]], groups, gates(name + "_pack"))
            link(token)
            flight[name + "_near"] = flight[name + "_far"] = [home(one, flip) for flip, one in enumerate(packed)]
            return
        near = out[:2]
        if style == "gated":
            near, token = pack(ids, quarter, near, [[(0, 0)], [(1, 0)]], gates(name + "_pack"))
            link(token)
        flight[name + "_near"] = [home(one, flip) for flip, one in enumerate(near)]
        far = flight[name + "_X"]
        if KNOBS.get("far_" + name, False):
            far, token = pack(ids, quarter, far, [[(0, 0)], [(1, 0)]], gates(name + "_far_pack"))
            link(token)
        flight[name + "_far"] = [home(one, flip) for flip, one in enumerate(far)]

    def finish(name):
        if KNOBS.get("out_" + name, "direct") == "packed":
            pieces, places = flight[name + "_near"], by_flip
        else:
            pieces, places = flight[name + "_near"] + flight[name + "_far"], by_row
        (whole,), token = put(ids, pieces, places, gates("put_" + name))
        link(token)
        return whole.reshape(-1)

    upper, middle = list(range(side + 1, side + row_bits)), list(range(1, top))
    singles = [[bit] for bit in middle[1:]]
    order = {
        "y,x,zz": [upper, [side], *singles, middle[:1] + [top]],
        "y,x,z,z": [upper, [side], *singles, middle[:1], [top]],
        "y,xz,z": [upper, [side] + middle[:1], *singles, [top]],
        "y,z,xz": [upper, middle[:1], *singles, [side, top]],
        "yx,zz": [upper + [side], *singles, middle[:1] + [top]],
        "yx,z,z": [upper + [side], *singles, middle[:1], [top]],
        "y,xzz": [upper, *singles, [side] + middle[:1] + [top]],
    }[KNOBS.get("order", "y,x,zz")]
    everything = sorted((bit for group in order for bit in group), reverse=True)
    sums = {}

    def begin(key, extra):
        keep, *send = extra
        sums[key] = keep, [across_core(one) for one in send], everything, 0

    def step(keys):
        known = [keys] if keys in sums else list(keys)
        _, _, left, n = sums[known[0]]
        name = "F%s_%d" % (keys, n)
        group = order[n]
        parts = [sums[key][:2] for key in known]
        own, pieces, flips, token = fold(ids, parts, len(keys) // len(known), left, group, unit, gates(name), work(name))
        link(token)
        come = [sent(one, lambda i, flip=flip: i ^ flip) for one, flip in zip(pieces, flips, strict=True)]
        flight[name] = come
        sums[keys] = own, come, [bit for bit in left if bit not in group], n + 1

    results = {}
    f_mid, (f_start,) = first_gate("G1f", forward_in, forward_place)
    f_out, (f_moved,) = second_gate("G2f", f_mid)
    cross("f", f_out)
    leave("f", f_out)
    a_mid, extra = first_gate("GE1", adjoint_in, adjoint_place, (f_start, first_from, unit, scale))
    begin("1", extra)
    for name in KNOBS["plan"]:
        if name == "G":
            a_out, extra = second_gate("GE2", a_mid, (f_moved, second_out, unit, scale))
            begin("2", extra)
            cross("a", a_out)
        elif name == "p":
            leave("a", a_out)
        elif name in "12":
            step(name)
        elif name == "J":
            while "12" not in sums and sums["2"][3] < len(order) - 1:
                step("1")
                step("2")
            step("12")
        elif name == "E":
            (env_one, env_two), token = add_up(ids, *sums["12"][:2], 2, gates("end"))
            link(token)
        else:
            results[name] = finish(name)
    return results["f"], results["a"], env_one.reshape(-1), env_two.reshape(-1)


def solution(mesh):
    in_specs = (P(AXES), P(AXES), P())
    out_specs = (P(AXES),) * 4
    return jax.shard_map(on_device, mesh=mesh, in_specs=in_specs, out_specs=out_specs, check_vma=False)
```
